32 devices in a mesh: section: 4 (over z), dp: 2 (over y), tensor: 4 (over x, core).
Axes of the slice: x: 2, y: 2, z: 4, core: 2. Of those that a mesh axis runs over, the one named last changes fastest.
Arguments:
- context: bfloat16 [4, 1024, 8192], P('section', 'dp', 'tensor'), may hold values from -6 to 6
- residual: bfloat16 [4, 1024, 8192], P('section', 'tensor', 'dp')
- out_weight: bfloat16 [4, 8192, 8192], P('section', 'tensor', 'dp'), may hold values from -0.0625 to 0.0625
- norm_gain: float32 [4, 8192], P('section'), may hold values from 0.25 to 1.75
- valid_tokens: int32 [4], P('section'), may hold values from 512 to 1024, as said below
Outputs:
- normed: bfloat16 [4, 1024, 8192], P('section', 'tensor', 'dp')
- handoff: bfloat16 [4, 1024, 8192], P('section', 'tensor', 'dp')
The draws below stay inside these ranges and needn't reach their ends.
Inputs may be any that keep to these rules, and one draw needn't show every extreme that they name: `valid_tokens`: some section's micro-batch is full in every draw.
All inputs are finite; a program needn't handle non-finite values.
Results may differ from the reference program's by a relative error of at most 0.018.
Values may be sent and summed in bfloat16 or wider, within the bound.
A program may use at most 64 MiB of HBM per device.

```python
import jax
import jax.numpy as jnp
from jax import lax

D = 8192
TOKS = 1024
N_SECTION = 4
N_TENSOR = 4


def draw_residual(key, part):
    key = jax.random.fold_in(key, 11)
    key_val, key_row = jax.random.split(key, 2)
    values = jax.random.normal(key_val, (N_SECTION, TOKS, D), jnp.float32)
    row_exp = jax.random.uniform(key_row, (N_SECTION, TOKS, 1), jnp.float32, -0.5, 0.5)
    col_exp = jnp.arange(D, dtype=jnp.float32)[None, None, :] / D - 0.5
    return (values * 10.0 ** row_exp * 10.0 ** col_exp).astype(jnp.bfloat16)


def draw_valid_tokens(key, part):
    key = jax.random.fold_in(key, 23)
    key_len, key_full = jax.random.split(key)
    lengths = jax.random.randint(key_len, (N_SECTION,), TOKS // 2, TOKS + 1)
    full = jax.random.randint(key_full, (), 0, N_SECTION)
    return lengths.at[full].set(TOKS).astype(jnp.int32)


def block_scale(key, extent, pieces, smallest, largest):
    level = 1.0
    for dim, shards_of in pieces:
        steps = jax.random.uniform(jax.random.fold_in(jax.random.fold_in(key, 6), dim), (shards_of,), jnp.float32, smallest / len(pieces), largest / len(pieces))
        level = level * jnp.repeat(jnp.exp(steps), extent[dim] // shards_of).reshape((-1,) + (1,) * (len(extent) - 1 - dim))
    return level


def bell_draw(key, shape, spread, most, cuts=(), held_as=jnp.bfloat16):
    entries = spread * jax.random.normal(key, shape, jnp.float32)
    if cuts:
        entries = entries * block_scale(key, shape, cuts, -0.22, 0.18)
    return jnp.clip(entries, -most, most).astype(held_as)


def setup_inputs(seed: int = 0) -> dict:
    seeds = jax.random.split(jax.random.key(seed), 6)
    return {
        "context": bell_draw(seeds[0], (N_SECTION, TOKS, D), 1.0, 6.0, ((0, 4), (1, 2), (2, 4))),
        "residual": draw_residual(jax.random.fold_in(seeds[5], 71), 0),
        "out_weight": bell_draw(seeds[2], (N_SECTION, D, D), D ** -0.5, 0.0625, ((0, 4), (1, 4), (2, 2))),
        "norm_gain": jnp.clip(1.0 + 0.15 * jax.random.normal(seeds[3], (N_SECTION, D), jnp.float32), 0.25, 1.75),
        "valid_tokens": draw_valid_tokens(jax.random.fold_in(seeds[5], 71), 0),
    }


def one_section(inputs):
    context_s, residual_s, weight_s, gain_s, valid_s = inputs
    width = D // N_TENSOR
    groups = context_s.reshape(TOKS, N_TENSOR, width).transpose(1, 0, 2)
    weights = weight_s.reshape(N_TENSOR, width, D)

    def add_group(total, pair):
        part = jnp.dot(pair[0], pair[1], preferred_element_type=jnp.float32).astype(jnp.bfloat16)
        part = lax.optimization_barrier(part)
        return (total + part.astype(jnp.float32), None)
    attn, _ = lax.scan(add_group, jnp.zeros((TOKS, D), jnp.float32), (groups, weights))
    hidden = residual_s.astype(jnp.float32) + attn
    mean_sq = lax.optimization_barrier(jnp.mean(hidden * hidden, axis=1, keepdims=True))
    keep = (jnp.arange(TOKS, dtype=jnp.int32) < valid_s)[:, None]
    normed = jnp.where(keep, hidden * lax.rsqrt(mean_sq + 1e-06) * gain_s[None, :], 0.0).astype(jnp.bfloat16)
    outgoing = jnp.where(keep, hidden, 0.0).astype(jnp.bfloat16)
    return (normed, outgoing)

def reference(context, residual, out_weight, norm_gain, valid_tokens):
    normed, outgoing = lax.map(one_section, (context, residual, out_weight, norm_gain, valid_tokens))
    handoff = jnp.concatenate([jnp.zeros_like(outgoing[:1]), outgoing[:-1]], axis=0)
    return (normed, handoff)
```

```python
import functools

import jax
import jax.numpy as jnp
from jax import lax
from jax.experimental import pallas as pl
from jax.experimental.pallas import tpu as pltpu
from jax.sharding import PartitionSpec as P

MESH = pl.DeviceIdType.MESH
PIECES = 8
AHEAD = 2
LAG = 2


def relay_kernel(
    sizes, valid_ref, context, residual, weight, gain, normed, handoff,
    rows_all, held_w, held_res, mine, pair_out, pair_in, chip_out, chip_in,
    hidden, passed, scaled, sq_out, sq_in,
    ctx_sem, w_sem, res_sem, y_send, y_recv, pair_send, pair_recv,
    chip_send, chip_recv, z_send, z_recv, sq_send, sq_recv, out_sem, zero_sem,
):
    sections, dps, chips, blocks, rows, depth, cols, r, steps, tile = sizes
    tiles = cols // tile
    sec = lax.axis_index("section")
    dp = lax.axis_index("dp")
    tensor = lax.axis_index("tensor")
    core = lax.rem(tensor, 2)
    chip = lax.div(tensor, 2)
    sibling = tensor + 1 - 2 * core
    dp_at = [lax.rem(dp + j, dps) for j in range(1, dps)]
    chip_at = [lax.rem(chip + j, chips) for j in range(1, chips)]

    def span(k):
        return pl.ds(pl.multiple_of(k * r, r), r)

    own = pl.ds(dp * blocks, blocks)
    ctx_load = pltpu.make_async_copy(context, rows_all.at[own], ctx_sem)
    ctx_load.start()

    def w_load(n):
        at = pl.ds(pl.multiple_of(n * tile, tile), tile)
        return pltpu.make_async_copy(weight.at[:, at], held_w.at[:, at], w_sem.at[n])

    def w_start(n, carry):
        w_load(n).start()
        return carry

    lax.fori_loop(0, tiles, w_start, 0)
    res_load = pltpu.make_async_copy(residual, held_res, res_sem)
    res_load.start()

    barrier = pltpu.get_barrier_semaphore()
    for d in dp_at:
        pl.semaphore_signal(barrier, inc=1, device_id={"dp": d}, device_id_type=MESH)
    pl.semaphore_signal(barrier, inc=1, device_id={"tensor": sibling}, device_id_type=MESH)
    for q in chip_at:
        pl.semaphore_signal(barrier, inc=1, device_id={"tensor": q * 2 + core}, device_id_type=MESH)

    @pl.when(sec > 0)
    def _():
        pl.semaphore_signal(barrier, inc=1, device_id={"section": sec - 1}, device_id_type=MESH)

    @pl.when(sec < sections - 1)
    def _():
        pl.semaphore_signal(barrier, inc=1, device_id={"section": sec + 1}, device_id_type=MESH)

    inner = (sec > 0) & (sec < sections - 1)

    @pl.when(inner)
    def _():
        pl.semaphore_wait(barrier, dps + chips + 1)

    @pl.when(jnp.logical_not(inner))
    def _():
        pl.semaphore_wait(barrier, dps + chips)

    def y_copy(k, j):
        return pltpu.make_async_remote_copy(
            src_ref=context.at[:, :, span(k), :],
            dst_ref=rows_all.at[own, :, span(k), :],
            send_sem=y_send.at[k, j],
            recv_sem=y_recv.at[k, j],
            device_id={"dp": dp_at[j]},
            device_id_type=MESH,
        )

    def pair_copy(k):
        return pltpu.make_async_remote_copy(
            src_ref=pair_out.at[k],
            dst_ref=pair_in.at[k],
            send_sem=pair_send.at[k],
            recv_sem=pair_recv.at[k],
            device_id={"tensor": sibling},
            device_id_type=MESH,
        )

    def chip_copy(k, j):
        return pltpu.make_async_remote_copy(
            src_ref=chip_out.at[j, span(k), :],
            dst_ref=chip_in.at[j, span(k), :],
            send_sem=chip_send.at[k, j],
            recv_sem=chip_recv.at[k, j],
            device_id={"tensor": chip_at[j] * 2 + core},
            device_id_type=MESH,
        )

    def z_copy(k):
        return pltpu.make_async_remote_copy(
            src_ref=passed.at[span(k), :],
            dst_ref=handoff.at[span(k), :],
            send_sem=z_send.at[k],
            recv_sem=z_recv.at[k],
            device_id={"section": lax.rem(sec + 1, sections)},
            device_id_type=MESH,
        )

    def sq_copy(k, j):
        return pltpu.make_async_remote_copy(
            src_ref=sq_out.at[k],
            dst_ref=sq_in.at[j, k],
            send_sem=sq_send.at[k, j],
            recv_sem=sq_recv.at[k, j],
            device_id={"dp": dp_at[j]},
            device_id_type=MESH,
        )

    def out_copy(k):
        return pltpu.make_async_copy(
            scaled.at[span(k), :], normed.at[span(k), :], out_sem.at[k]
        )

    def zero_copy(k):
        return pltpu.make_async_copy(
            passed.at[span(0), :], handoff.at[span(k), :], zero_sem.at[k]
        )

    for k in range(min(AHEAD, steps)):
        for j in range(dps - 1):
            y_copy(k, j).start()

    @pl.when(sec == 0)
    def _():
        passed[span(0), :] = jnp.zeros((r, cols), passed.dtype)

        def begin(k, carry):
            zero_copy(k).start()
            return carry

        def finish(k, carry):
            zero_copy(k).wait()
            return carry

        lax.fori_loop(0, steps, begin, 0)
        lax.fori_loop(0, steps, finish, 0)

    ctx_load.wait()
    half = chips * r

    def product(k):
        for j in range(dps - 1):
            y_copy(k, j).wait_recv()

        @pl.when(k + AHEAD < steps)
        def _():
            for j in range(dps - 1):
                y_copy(k + AHEAD, j).start()

        def one_tile(n, carry):
            @pl.when(k == 0)
            def _():
                w_load(n).wait()

            at = pl.ds(pl.multiple_of(n * tile, tile), tile)
            lhs = jnp.concatenate(
                [rows_all[:, 1 - core, span(k), :], rows_all[:, core, span(k), :]], axis=0
            ).reshape(2 * half, depth)
            part = jnp.dot(lhs, held_w[:, at], preferred_element_type=jnp.float32)
            pair_out[k, :, :, at] = part[:half].astype(jnp.bfloat16).reshape(chips, r, tile)
            mine[:, :, at] = part[half:].reshape(chips, r, tile)
            return carry

        lax.fori_loop(0, tiles, one_tile, 0)
        pair_copy(k).start()

    def combine(k):
        pair_copy(k).wait_recv()
        for j in range(chips - 1):
            both = mine[chip_at[j]] + pair_in[k, chip_at[j]].astype(jnp.float32)
            chip_out[j, span(k), :] = both.astype(jnp.bfloat16)
            chip_copy(k, j).start()
        both = mine[chip] + pair_in[k, chip].astype(jnp.float32)
        hidden[span(k), :] = both

    def row_mask(k):
        ids = tensor * rows + k * r + lax.broadcasted_iota(jnp.int32, (r, 1), 0)
        return ids < valid_ref[0]

    def add_residual(k):
        @pl.when(k == 0)
        def _():
            res_load.wait()

        for j in range(chips - 1):
            chip_copy(k, j).wait_recv()
        keep = row_mask(k)
        total = jnp.zeros((r, 128), jnp.float32)
        for n in range(tiles):
            at = pl.ds(n * tile, tile)
            h = hidden[span(k), at]
            for j in range(chips - 1):
                h = h + chip_in[j, span(k), at].astype(jnp.float32)
            h = h + held_res[span(k), at].astype(jnp.float32)
            hidden[span(k), at] = h
            passed[span(k), at] = jnp.where(keep, h, 0.0).astype(jnp.bfloat16)
            sq = h * h
            for c in range(tile // 128):
                total = total + sq[:, c * 128 : (c + 1) * 128]
        sq_out[k] = total
        for j in range(dps - 1):
            sq_copy(k, j).start()

        @pl.when(sec < sections - 1)
        def _():
            z_copy(k).start()

    def normalize(k):
        total = sq_out[k]
        for j in range(dps - 1):
            sq_copy(k, j).wait_recv()
            total = total + sq_in[j, k]
        mean_sq = jnp.sum(total, axis=1, keepdims=True) / (dps * cols)
        scale = jnp.where(row_mask(k), lax.rsqrt(mean_sq + 1e-06), 0.0)
        for n in range(tiles):
            at = pl.ds(n * tile, tile)
            g = gain[:, pl.ds(pl.multiple_of(dp * cols + n * tile, tile), tile)]
            scaled[span(k), at] = (hidden[span(k), at] * scale * g).astype(jnp.bfloat16)
        out_copy(k).start()

    def step(s, carry):
        @pl.when(s < steps)
        def _():
            product(s)

        @pl.when(s > LAG)
        def _():
            normalize(s - LAG - 1)

        @pl.when(s < steps)
        def _():
            combine(s)

        @pl.when((s >= LAG) & (s < steps + LAG))
        def _():
            add_residual(s - LAG)

        return carry

    lax.fori_loop(0, steps + LAG + 1, step, 0)

    def drain(k, carry):
        for j in range(dps - 1):
            y_copy(k, j).wait_send()
            sq_copy(k, j).wait_send()
        pair_copy(k).wait_send()
        for j in range(chips - 1):
            chip_copy(k, j).wait_send()
        out_copy(k).wait()

        @pl.when(sec < sections - 1)
        def _():
            z_copy(k).wait_send()

        @pl.when(sec > 0)
        def _():
            z_copy(k).wait_recv()

        return carry

    lax.fori_loop(0, steps, drain, 0)


def on_device(context, residual, out_weight, norm_gain, valid_tokens):
    sections, dps, tensors = (lax.axis_size(a) for a in ("section", "dp", "tensor"))
    chips = tensors // 2
    rows, cols = residual.shape[1:]
    local, depth = context.shape[1:]
    blocks = local // (2 * rows)
    assert blocks * dps == chips
    r = max(16, rows // PIECES)
    steps = rows // r
    tile = min(512, cols)
    sizes = (sections, dps, chips, blocks, rows, depth, cols, r, steps, tile)
    bf16, f32 = jnp.bfloat16, jnp.float32
    dma = pltpu.SemaphoreType.DMA
    total_rows = local * dps
    anywhere = pl.BlockSpec(memory_space=pl.ANY)
    out = jax.ShapeDtypeStruct((rows, cols), bf16)
    normed, handoff = pl.pallas_call(
        functools.partial(relay_kernel, sizes),
        out_shape=(out, out),
        in_specs=[
            pl.BlockSpec(memory_space=pltpu.SMEM),
            anywhere,
            anywhere,
            anywhere,
            pl.BlockSpec(memory_space=pltpu.VMEM),
        ],
        out_specs=(anywhere, anywhere),
        scratch_shapes=[
            pltpu.VMEM((chips, 2, rows, depth), bf16),
            pltpu.VMEM((depth, cols), bf16),
            pltpu.VMEM((rows, cols), bf16),
            pltpu.VMEM((chips, r, cols), f32),
            pltpu.VMEM((steps, chips, r, cols), bf16),
            pltpu.VMEM((steps, chips, r, cols), bf16),
            pltpu.VMEM((chips - 1, rows, cols), bf16),
            pltpu.VMEM((chips - 1, rows, cols), bf16),
            pltpu.VMEM((rows, cols), f32),
            pltpu.VMEM((rows, cols), bf16),
            pltpu.VMEM((rows, cols), bf16),
            pltpu.VMEM((steps, r, 128), f32),
            pltpu.VMEM((dps - 1, steps, r, 128), f32),
            dma,
            dma((cols // tile,)),
            dma,
            dma((steps, dps - 1)),
            dma((steps, dps - 1)),
            dma((steps,)),
            dma((steps,)),
            dma((steps, chips - 1)),
            dma((steps, chips - 1)),
            dma((steps,)),
            dma((steps,)),
            dma((steps, dps - 1)),
            dma((steps, dps - 1)),
            dma((steps,)),
            dma((steps,)),
        ],
        compiler_params=pltpu.CompilerParams(
            collective_id=0, has_side_effects=True, vmem_limit_bytes=56 * 2**20
        ),
        cost_estimate=pl.CostEstimate(
            flops=2 * total_rows * depth * cols,
            bytes_accessed=2 * (depth * cols + local * depth + 3 * rows * cols),
            transcendentals=0,
        ),
        name="relay",
    )(
        valid_tokens,
        context.reshape(blocks, 2, rows, depth),
        residual[0],
        out_weight[0],
        norm_gain,
    )
    return (normed[None], handoff[None])


def solution(mesh):
    placed = (
        P("section", "dp", "tensor"),
        P("section", "tensor", "dp"),
        P("section", "tensor", "dp"),
        P("section", None),
        P("section"),
    )
    return jax.shard_map(
        on_device,
        mesh=mesh,
        in_specs=placed,
        out_specs=(P("section", "tensor", "dp"), P("section", "tensor", "dp")),
        check_vma=False,
    )
```

```python
import functools

import jax
import jax.numpy as jnp
from jax import lax
from jax.experimental import pallas as pl
from jax.experimental.pallas import tpu as pltpu
from jax.sharding import PartitionSpec as P

MESH = pl.DeviceIdType.MESH
PIECES = 8
AHEAD = 2
LAG = 2
GROUPS = 4


def relay_kernel(
    sizes, valid_ref, context, residual, weight, gain, normed, handoff,
    rows_all, lhs, held_w, held_res, mine, pair_out, pair_in, chip_out, chip_in,
    hidden, passed, scaled, sq_out, sq_in,
    ctx_sem, w_sem, res_sem, y_send, y_recv, pair_send, pair_recv,
    chip_send, chip_recv, z_send, z_recv, sq_send, sq_recv, out_sem, zero_sem,
):
    sections, dps, chips, blocks, rows, depth, cols, r, steps, tile = sizes
    tiles = cols // tile
    half = chips * r
    sec = lax.axis_index("section")
    dp = lax.axis_index("dp")
    tensor = lax.axis_index("tensor")
    core = lax.rem(tensor, 2)
    chip = lax.div(tensor, 2)
    sibling = tensor + 1 - 2 * core
    dp_at = [lax.rem(dp + j, dps) for j in range(1, dps)]
    chip_at = [lax.rem(chip + j, chips) for j in range(1, chips)]

    def span(k):
        return pl.ds(pl.multiple_of(k * r, r), r)

    own = pl.ds(dp * blocks, blocks)
    ctx_load = pltpu.make_async_copy(context, rows_all.at[own], ctx_sem)
    ctx_load.start()

    def group(n):
        return pl.ds(n * tile, tile)

    def w_load(n):
        at = group(n)
        return pltpu.make_async_copy(weight.at[:, at], held_w.at[:, at], w_sem.at[n])

    for n in range(tiles):
        w_load(n).start()
    res_load = pltpu.make_async_copy(residual, held_res, res_sem)
    res_load.start()

    barrier = pltpu.get_barrier_semaphore()
    for d in dp_at:
        pl.semaphore_signal(barrier, inc=1, device_id={"dp": d}, device_id_type=MESH)
    pl.semaphore_signal(barrier, inc=1, device_id={"tensor": sibling}, device_id_type=MESH)
    for q in chip_at:
        pl.semaphore_signal(barrier, inc=1, device_id={"tensor": q * 2 + core}, device_id_type=MESH)

    @pl.when(sec > 0)
    def _():
        pl.semaphore_signal(barrier, inc=1, device_id={"section": sec - 1}, device_id_type=MESH)

    @pl.when(sec < sections - 1)
    def _():
        pl.semaphore_signal(barrier, inc=1, device_id={"section": sec + 1}, device_id_type=MESH)

    inner = (sec > 0) & (sec < sections - 1)

    @pl.when(inner)
    def _():
        pl.semaphore_wait(barrier, dps + chips + 1)

    @pl.when(jnp.logical_not(inner))
    def _():
        pl.semaphore_wait(barrier, dps + chips)

    def y_copy(k, j):
        return pltpu.make_async_remote_copy(
            src_ref=context.at[:, :, span(k), :],
            dst_ref=rows_all.at[own, :, span(k), :],
            send_sem=y_send.at[k, j],
            recv_sem=y_recv.at[k, j],
            device_id={"dp": dp_at[j]},
            device_id_type=MESH,
        )

    def pair_copy(k, n):
        return pltpu.make_async_remote_copy(
            src_ref=pair_out.at[k, :, :, group(n)],
            dst_ref=pair_in.at[k, :, :, group(n)],
            send_sem=pair_send.at[k, n],
            recv_sem=pair_recv.at[k, n],
            device_id={"tensor": sibling},
            device_id_type=MESH,
        )

    def chip_copy(k, n, j):
        return pltpu.make_async_remote_copy(
            src_ref=chip_out.at[j, span(k), group(n)],
            dst_ref=chip_in.at[j, span(k), group(n)],
            send_sem=chip_send.at[k, n, j],
            recv_sem=chip_recv.at[k, n, j],
            device_id={"tensor": chip_at[j] * 2 + core},
            device_id_type=MESH,
        )

    def z_copy(k, n):
        return pltpu.make_async_remote_copy(
            src_ref=passed.at[span(k), group(n)],
            dst_ref=handoff.at[span(k), group(n)],
            send_sem=z_send.at[k, n],
            recv_sem=z_recv.at[k, n],
            device_id={"section": lax.rem(sec + 1, sections)},
            device_id_type=MESH,
        )

    def sq_copy(k, j):
        return pltpu.make_async_remote_copy(
            src_ref=sq_out.at[k],
            dst_ref=sq_in.at[j, k],
            send_sem=sq_send.at[k, j],
            recv_sem=sq_recv.at[k, j],
            device_id={"dp": dp_at[j]},
            device_id_type=MESH,
        )

    def out_copy(k):
        return pltpu.make_async_copy(
            scaled.at[span(k), :], normed.at[span(k), :], out_sem.at[k]
        )

    def zero_copy(k):
        return pltpu.make_async_copy(
            passed.at[span(0), :], handoff.at[span(k), :], zero_sem.at[k]
        )

    for k in range(min(AHEAD, steps)):
        for j in range(dps - 1):
            y_copy(k, j).start()

    @pl.when(sec == 0)
    def _():
        passed[span(0), :] = jnp.zeros((r, cols), passed.dtype)

        def begin(k, carry):
            zero_copy(k).start()
            return carry

        def finish(k, carry):
            zero_copy(k).wait()
            return carry

        lax.fori_loop(0, steps, begin, 0)
        lax.fori_loop(0, steps, finish, 0)

    ctx_load.wait()

    def gather(k):
        for j in range(dps - 1):
            y_copy(k, j).wait_recv()

        @pl.when(k + AHEAD < steps)
        def _():
            for j in range(dps - 1):
                y_copy(k + AHEAD, j).start()

        for q in range(chips):
            lhs[pl.ds(q * r, r), :] = rows_all[q, 1 - core, span(k), :]
            lhs[pl.ds(half + q * r, r), :] = rows_all[q, core, span(k), :]

    def product(k, n):
        @pl.when(k == 0)
        def _():
            w_load(n).wait()

        part = jnp.dot(lhs[...], held_w[:, group(n)], preferred_element_type=jnp.float32)
        pair_out[k, :, :, group(n)] = part[:half].astype(jnp.bfloat16).reshape(chips, r, tile)
        mine[:, :, group(n)] = part[half:].reshape(chips, r, tile)
        pair_copy(k, n).start()

    def combine(k, n):
        pair_copy(k, n).wait_recv()

        def pair_sum(q):
            return mine[q, :, group(n)] + pair_in[k, q, :, group(n)].astype(jnp.float32)

        for j in range(chips - 1):
            chip_out[j, span(k), group(n)] = pair_sum(chip_at[j]).astype(jnp.bfloat16)
            chip_copy(k, n, j).start()
        hidden[span(k), group(n)] = pair_sum(chip)

    def row_mask(k):
        ids = tensor * rows + k * r + lax.broadcasted_iota(jnp.int32, (r, 1), 0)
        return ids < valid_ref[0]

    def add_residual(k):
        @pl.when(k == 0)
        def _():
            res_load.wait()

        keep = row_mask(k)
        total = jnp.zeros((r, 128), jnp.float32)
        for n in range(tiles):
            at = group(n)
            for j in range(chips - 1):
                chip_copy(k, n, j).wait_recv()
            h = hidden[span(k), at]
            for j in range(chips - 1):
                h = h + chip_in[j, span(k), at].astype(jnp.float32)
            h = h + held_res[span(k), at].astype(jnp.float32)
            hidden[span(k), at] = h
            passed[span(k), at] = jnp.where(keep, h, 0.0).astype(jnp.bfloat16)

            @pl.when(sec < sections - 1)
            def _():
                z_copy(k, n).start()

            sq = h * h
            for c in range(tile // 128):
                total = total + sq[:, c * 128 : (c + 1) * 128]
        sq_out[k] = total
        for j in range(dps - 1):
            sq_copy(k, j).start()

    def normalize(k):
        total = sq_out[k]
        for j in range(dps - 1):
            sq_copy(k, j).wait_recv()
            total = total + sq_in[j, k]
        mean_sq = jnp.sum(total, axis=1, keepdims=True) / (dps * cols)
        scale = jnp.where(row_mask(k), lax.rsqrt(mean_sq + 1e-06), 0.0)
        for n in range(tiles):
            at = pl.ds(n * tile, tile)
            g = gain[:, pl.ds(pl.multiple_of(dp * cols + n * tile, tile), tile)]
            scaled[span(k), at] = (hidden[span(k), at] * scale * g).astype(jnp.bfloat16)
        out_copy(k).start()

    def step(s, carry):
        @pl.when(s < steps)
        def _():
            gather(s)
            product(s, 0)
            for n in range(1, tiles):
                product(s, n)
                combine(s, n - 1)

        @pl.when(s > LAG)
        def _():
            normalize(s - LAG - 1)

        @pl.when(s < steps)
        def _():
            combine(s, tiles - 1)

        @pl.when((s >= LAG) & (s < steps + LAG))
        def _():
            add_residual(s - LAG)

        return carry

    lax.fori_loop(0, steps + LAG + 1, step, 0)

    def drain(k, carry):
        for j in range(dps - 1):
            y_copy(k, j).wait_send()
            sq_copy(k, j).wait_send()
        out_copy(k).wait()
        for n in range(tiles):
            pair_copy(k, n).wait_send()
            for j in range(chips - 1):
                chip_copy(k, n, j).wait_send()

        @pl.when(sec < sections - 1)
        def _():
            for n in range(tiles):
                z_copy(k, n).wait_send()

        @pl.when(sec > 0)
        def _():
            for n in range(tiles):
                z_copy(k, n).wait_recv()

        return carry

    lax.fori_loop(0, steps, drain, 0)


def on_device(context, residual, out_weight, norm_gain, valid_tokens):
    sections, dps, tensors = (lax.axis_size(a) for a in ("section", "dp", "tensor"))
    chips = tensors // 2
    rows, cols = residual.shape[1:]
    local, depth = context.shape[1:]
    blocks = local // (2 * rows)
    assert blocks * dps == chips
    r = max(16, rows // PIECES)
    steps = rows // r
    tile = cols // GROUPS
    tiles = GROUPS
    sizes = (sections, dps, chips, blocks, rows, depth, cols, r, steps, tile)
    bf16, f32 = jnp.bfloat16, jnp.float32
    dma = pltpu.SemaphoreType.DMA
    total_rows = local * dps
    anywhere = pl.BlockSpec(memory_space=pl.ANY)
    out = jax.ShapeDtypeStruct((rows, cols), bf16)
    normed, handoff = pl.pallas_call(
        functools.partial(relay_kernel, sizes),
        out_shape=(out, out),
        in_specs=[
            pl.BlockSpec(memory_space=pltpu.SMEM),
            anywhere,
            anywhere,
            anywhere,
            pl.BlockSpec(memory_space=pltpu.VMEM),
        ],
        out_specs=(anywhere, anywhere),
        scratch_shapes=[
            pltpu.VMEM((chips, 2, rows, depth), bf16),
            pltpu.VMEM((2 * chips * r, depth), bf16),
            pltpu.VMEM((depth, cols), bf16),
            pltpu.VMEM((rows, cols), bf16),
            pltpu.VMEM((chips, r, cols), f32),
            pltpu.VMEM((steps, chips, r, cols), bf16),
            pltpu.VMEM((steps, chips, r, cols), bf16),
            pltpu.VMEM((chips - 1, rows, cols), bf16),
            pltpu.VMEM((chips - 1, rows, cols), bf16),
            pltpu.VMEM((rows, cols), f32),
            pltpu.VMEM((rows, cols), bf16),
            pltpu.VMEM((rows, cols), bf16),
            pltpu.VMEM((steps, r, 128), f32),
            pltpu.VMEM((dps - 1, steps, r, 128), f32),
            dma,
            dma((tiles,)),
            dma,
            dma((steps, dps - 1)),
            dma((steps, dps - 1)),
            dma((steps, tiles)),
            dma((steps, tiles)),
            dma((steps, tiles, chips - 1)),
            dma((steps, tiles, chips - 1)),
            dma((steps, tiles)),
            dma((steps, tiles)),
            dma((steps, dps - 1)),
            dma((steps, dps - 1)),
            dma((steps,)),
            dma((steps,)),
        ],
        compiler_params=pltpu.CompilerParams(
            collective_id=0, has_side_effects=True, vmem_limit_bytes=56 * 2**20
        ),
        cost_estimate=pl.CostEstimate(
            flops=2 * total_rows * depth * cols,
            bytes_accessed=2 * (depth * cols + local * depth + 3 * rows * cols),
            transcendentals=0,
        ),
        name="relay",
    )(
        valid_tokens,
        context.reshape(blocks, 2, rows, depth),
        residual[0],
        out_weight[0],
        norm_gain,
    )
    return (normed[None], handoff[None])


def solution(mesh):
    placed = (
        P("section", "dp", "tensor"),
        P("section", "tensor", "dp"),
        P("section", "tensor", "dp"),
        P("section", None),
        P("section"),
    )
    return jax.shard_map(
        on_device,
        mesh=mesh,
        in_specs=placed,
        out_specs=(P("section", "tensor", "dp"), P("section", "tensor", "dp")),
        check_vma=False,
    )
```

```python
import functools

import jax
import jax.numpy as jnp
from jax import lax
from jax.experimental import pallas as pl
from jax.experimental.pallas import tpu as pltpu
from jax.sharding import PartitionSpec as P

MESH = pl.DeviceIdType.MESH
PIECES = 8
GROUPS = 4


def relay_kernel(
    sizes, valid_ref, context, residual, weight, gain, normed, handoff,
    rows_all, lhs, held_w, held_res, mine, pair_out, pair_in, chip_out, chip_in,
    hidden, passed, scaled, sq_out, sq_in,
    ctx_sem, w_sem, res_sem, y_send, y_recv, pair_send, pair_recv,
    chip_send, chip_recv, z_send, z_recv, sq_send, sq_recv, out_sem, zero_sem,
):
    sections, dps, chips, blocks, rows, depth, cols, r, steps, tile = sizes
    tiles = cols // tile
    half = chips * r
    sec = lax.axis_index("section")
    dp = lax.axis_index("dp")
    tensor = lax.axis_index("tensor")
    core = lax.rem(tensor, 2)
    chip = lax.div(tensor, 2)
    sibling = tensor + 1 - 2 * core
    dp_at = [lax.rem(dp + j, dps) for j in range(1, dps)]
    chip_at = [lax.rem(chip + j, chips) for j in range(1, chips)]

    def span(k):
        return pl.ds(pl.multiple_of(k * r, r), r)

    own = pl.ds(dp * blocks, blocks)
    ctx_load = pltpu.make_async_copy(context, rows_all.at[own], ctx_sem)
    ctx_load.start()

    def group(n):
        return pl.ds(n * tile, tile)

    def w_load(n):
        at = group(n)
        return pltpu.make_async_copy(weight.at[:, at], held_w.at[:, at], w_sem.at[n])

    for n in range(tiles):
        w_load(n).start()
    res_load = pltpu.make_async_copy(residual, held_res, res_sem)
    res_load.start()

    barrier = pltpu.get_barrier_semaphore()
    for d in dp_at:
        pl.semaphore_signal(barrier, inc=1, device_id={"dp": d}, device_id_type=MESH)
    pl.semaphore_signal(barrier, inc=1, device_id={"tensor": sibling}, device_id_type=MESH)
    for q in chip_at:
        pl.semaphore_signal(barrier, inc=1, device_id={"tensor": q * 2 + core}, device_id_type=MESH)

    @pl.when(sec > 0)
    def _():
        pl.semaphore_signal(barrier, inc=1, device_id={"section": sec - 1}, device_id_type=MESH)

    @pl.when(sec < sections - 1)
    def _():
        pl.semaphore_signal(barrier, inc=1, device_id={"section": sec + 1}, device_id_type=MESH)

    inner = (sec > 0) & (sec < sections - 1)

    @pl.when(inner)
    def _():
        pl.semaphore_wait(barrier, dps + chips + 1)

    @pl.when(jnp.logical_not(inner))
    def _():
        pl.semaphore_wait(barrier, dps + chips)

    def y_copy(k, j):
        return pltpu.make_async_remote_copy(
            src_ref=context.at[:, :, span(k), :],
            dst_ref=rows_all.at[own, :, span(k), :],
            send_sem=y_send.at[k, j],
            recv_sem=y_recv.at[k, j],
            device_id={"dp": dp_at[j]},
            device_id_type=MESH,
        )

    def pair_copy(k, n):
        return pltpu.make_async_remote_copy(
            src_ref=pair_out.at[k, :, :, group(n)],
            dst_ref=pair_in.at[k, :, :, group(n)],
            send_sem=pair_send.at[k, n],
            recv_sem=pair_recv.at[k, n],
            device_id={"tensor": sibling},
            device_id_type=MESH,
        )

    def chip_copy(k, n, j):
        return pltpu.make_async_remote_copy(
            src_ref=chip_out.at[j, span(k), group(n)],
            dst_ref=chip_in.at[j, span(k), group(n)],
            send_sem=chip_send.at[k, n, j],
            recv_sem=chip_recv.at[k, n, j],
            device_id={"tensor": chip_at[j] * 2 + core},
            device_id_type=MESH,
        )

    def z_copy(k, n):
        return pltpu.make_async_remote_copy(
            src_ref=passed.at[span(k), group(n)],
            dst_ref=handoff.at[span(k), group(n)],
            send_sem=z_send.at[k, n],
            recv_sem=z_recv.at[k, n],
            device_id={"section": lax.rem(sec + 1, sections)},
            device_id_type=MESH,
        )

    def sq_copy(k, j):
        return pltpu.make_async_remote_copy(
            src_ref=sq_out.at[k],
            dst_ref=sq_in.at[j, k],
            send_sem=sq_send.at[k, j],
            recv_sem=sq_recv.at[k, j],
            device_id={"dp": dp_at[j]},
            device_id_type=MESH,
        )

    def out_copy(k):
        return pltpu.make_async_copy(
            scaled.at[span(k), :], normed.at[span(k), :], out_sem.at[k]
        )

    def zero_copy(k):
        return pltpu.make_async_copy(
            passed.at[span(0), :], handoff.at[span(k), :], zero_sem.at[k]
        )

    def y_start(k):
        for j in range(dps - 1):
            y_copy(k, j).start()

    y_start(0)

    @pl.when(sec == 0)
    def _():
        passed[span(0), :] = jnp.zeros((r, cols), passed.dtype)

        def begin(k, carry):
            zero_copy(k).start()
            return carry

        def finish(k, carry):
            zero_copy(k).wait()
            return carry

        lax.fori_loop(0, steps, begin, 0)
        lax.fori_loop(0, steps, finish, 0)

    for j in range(dps - 1):
        y_copy(0, j).wait_send()
    if steps > 1:
        y_start(1)
    ctx_load.wait()

    def gather(k):
        for j in range(dps - 1):
            y_copy(k, j).wait_recv()

        for q in range(chips):
            lhs[pl.ds(q * r, r), :] = rows_all[q, 1 - core, span(k), :]
            lhs[pl.ds(half + q * r, r), :] = rows_all[q, core, span(k), :]

    def product(k, n):
        @pl.when(k == 0)
        def _():
            w_load(n).wait()

        part = jnp.dot(lhs[...], held_w[:, group(n)], preferred_element_type=jnp.float32)
        pair_out[k, :, :, group(n)] = part[:half].astype(jnp.bfloat16).reshape(chips, r, tile)
        mine[:, :, group(n)] = part[half:].reshape(chips, r, tile)
        pair_copy(k, n).start()

    def combine(k, n):
        pair_copy(k, n).wait_recv()

        def pair_sum(q):
            return mine[q, :, group(n)] + pair_in[k, q, :, group(n)].astype(jnp.float32)

        for j in range(chips - 1):
            chip_out[j, span(k), group(n)] = pair_sum(chip_at[j]).astype(jnp.bfloat16)
            chip_copy(k, n, j).start()
        hidden[span(k), group(n)] = pair_sum(chip)

    def row_mask(k):
        ids = tensor * rows + k * r + lax.broadcasted_iota(jnp.int32, (r, 1), 0)
        return ids < valid_ref[0]

    def add_residual(k, n):
        if n == 0:

            @pl.when(k == 0)
            def _():
                res_load.wait()

        at = group(n)
        for j in range(chips - 1):
            chip_copy(k, n, j).wait_recv()
        h = hidden[span(k), at]
        for j in range(chips - 1):
            h = h + chip_in[j, span(k), at].astype(jnp.float32)
        h = h + held_res[span(k), at].astype(jnp.float32)
        hidden[span(k), at] = h
        passed[span(k), at] = jnp.where(row_mask(k), h, 0.0).astype(jnp.bfloat16)

        @pl.when(sec < sections - 1)
        def _():
            z_copy(k, n).start()

        sq = h * h
        total = sq[:, :128]
        for c in range(1, tile // 128):
            total = total + sq[:, c * 128 : (c + 1) * 128]
        sq_out[k] = total if n == 0 else sq_out[k] + total
        if n == tiles - 1:
            for j in range(dps - 1):
                sq_copy(k, j).start()

    def normalize(k):
        total = sq_out[k]
        for j in range(dps - 1):
            sq_copy(k, j).wait_recv()
            total = total + sq_in[j, k]
        mean_sq = jnp.sum(total, axis=1, keepdims=True) / (dps * cols)
        scale = jnp.where(row_mask(k), lax.rsqrt(mean_sq + 1e-06), 0.0)
        for n in range(tiles):
            at = pl.ds(n * tile, tile)
            g = gain[:, pl.ds(pl.multiple_of(dp * cols + n * tile, tile), tile)]
            scaled[span(k), at] = (hidden[span(k), at] * scale * g).astype(jnp.bfloat16)
        out_copy(k).start()

    def step(s, carry):
        @pl.when(s < steps)
        def _():
            gather(s)

        for n in range(tiles):

            @pl.when(s < steps)
            def _():
                product(s, n)
                if n > 0:
                    combine(s, n - 1)

            if n == max(0, tiles - 2):

                @pl.when(s + 2 < steps)
                def _():
                    y_start(s + 2)

            if n > 0:

                @pl.when((s > 0) & (s <= steps))
                def _():
                    add_residual(s - 1, n)

        @pl.when(s < steps)
        def _():
            combine(s, tiles - 1)
            add_residual(s, 0)

        @pl.when(s > 1)
        def _():
            normalize(s - 2)

        return carry

    lax.fori_loop(0, steps + 2, step, 0)

    def drain(k, carry):
        @pl.when(k > 0)
        def _():
            for j in range(dps - 1):
                y_copy(k, j).wait_send()

        for j in range(dps - 1):
            sq_copy(k, j).wait_send()
        out_copy(k).wait()
        for n in range(tiles):
            pair_copy(k, n).wait_send()
            for j in range(chips - 1):
                chip_copy(k, n, j).wait_send()

        @pl.when(sec < sections - 1)
        def _():
            for n in range(tiles):
                z_copy(k, n).wait_send()

        @pl.when(sec > 0)
        def _():
            for n in range(tiles):
                z_copy(k, n).wait_recv()

        return carry

    lax.fori_loop(0, steps, drain, 0)


def on_device(context, residual, out_weight, norm_gain, valid_tokens):
    sections, dps, tensors = (lax.axis_size(a) for a in ("section", "dp", "tensor"))
    chips = tensors // 2
    rows, cols = residual.shape[1:]
    local, depth = context.shape[1:]
    blocks = local // (2 * rows)
    assert blocks * dps == chips
    r = max(16, rows // PIECES)
    steps = rows // r
    tile = cols // GROUPS
    tiles = GROUPS
    sizes = (sections, dps, chips, blocks, rows, depth, cols, r, steps, tile)
    bf16, f32 = jnp.bfloat16, jnp.float32
    dma = pltpu.SemaphoreType.DMA
    total_rows = local * dps
    anywhere = pl.BlockSpec(memory_space=pl.ANY)
    out = jax.ShapeDtypeStruct((rows, cols), bf16)
    normed, handoff = pl.pallas_call(
        functools.partial(relay_kernel, sizes),
        out_shape=(out, out),
        in_specs=[
            pl.BlockSpec(memory_space=pltpu.SMEM),
            anywhere,
            anywhere,
            anywhere,
            pl.BlockSpec(memory_space=pltpu.VMEM),
        ],
        out_specs=(anywhere, anywhere),
        scratch_shapes=[
            pltpu.VMEM((chips, 2, rows, depth), bf16),
            pltpu.VMEM((2 * chips * r, depth), bf16),
            pltpu.VMEM((depth, cols), bf16),
            pltpu.VMEM((rows, cols), bf16),
            pltpu.VMEM((chips, r, cols), f32),
            pltpu.VMEM((steps, chips, r, cols), bf16),
            pltpu.VMEM((steps, chips, r, cols), bf16),
            pltpu.VMEM((chips - 1, rows, cols), bf16),
            pltpu.VMEM((chips - 1, rows, cols), bf16),
            pltpu.VMEM((rows, cols), f32),
            pltpu.VMEM((rows, cols), bf16),
            pltpu.VMEM((rows, cols), bf16),
            pltpu.VMEM((steps, r, 128), f32),
            pltpu.VMEM((dps - 1, steps, r, 128), f32),
            dma,
            dma((tiles,)),
            dma,
            dma((steps, dps - 1)),
            dma((steps, dps - 1)),
            dma((steps, tiles)),
            dma((steps, tiles)),
            dma((steps, tiles, chips - 1)),
            dma((steps, tiles, chips - 1)),
            dma((steps, tiles)),
            dma((steps, tiles)),
            dma((steps, dps - 1)),
            dma((steps, dps - 1)),
            dma((steps,)),
            dma((steps,)),
        ],
        compiler_params=pltpu.CompilerParams(
            collective_id=0, has_side_effects=True, vmem_limit_bytes=56 * 2**20
        ),
        cost_estimate=pl.CostEstimate(
            flops=2 * total_rows * depth * cols,
            bytes_accessed=2 * (depth * cols + local * depth + 3 * rows * cols),
            transcendentals=0,
        ),
        name="relay",
    )(
        valid_tokens,
        context.reshape(blocks, 2, rows, depth),
        residual[0],
        out_weight[0],
        norm_gain,
    )
    return (normed[None], handoff[None])


def solution(mesh):
    placed = (
        P("section", "dp", "tensor"),
        P("section", "tensor", "dp"),
        P("section", "tensor", "dp"),
        P("section", None),
        P("section"),
    )
    return jax.shard_map(
        on_device,
        mesh=mesh,
        in_specs=placed,
        out_specs=(P("section", "tensor", "dp"), P("section", "tensor", "dp")),
        check_vma=False,
    )
```

```python
import functools

import jax
import jax.numpy as jnp
from jax import lax
from jax.experimental import pallas as pl
from jax.experimental.pallas import tpu as pltpu
from jax.sharding import PartitionSpec as P

MESH = pl.DeviceIdType.MESH
PIECES = 8
GROUPS = 4


def relay_kernel(
    sizes, valid_ref, context, residual, weight, gain, normed, handoff,
    rows_all, lhs, held_w, held_res, mine, pair_out, pair_in, chip_out, chip_in,
    hidden, passed, sq_out, sq_in,
    ctx_sem, w_sem, res_sem, y_send, y_recv, pair_send, pair_recv,
    chip_send, chip_recv, z_send, z_recv, sq_send, sq_recv,
):
    sections, dps, chips, blocks, rows, depth, cols, r, steps, tile = sizes
    tiles = cols // tile
    half = chips * r
    first = (tiles + 1) // 2
    sec = lax.axis_index("section")
    dp = lax.axis_index("dp")
    tensor = lax.axis_index("tensor")
    core = lax.rem(tensor, 2)
    chip = lax.div(tensor, 2)
    sibling = tensor + 1 - 2 * core
    dp_at = [lax.rem(dp + j, dps) for j in range(1, dps)]
    chip_at = [lax.rem(chip + j, chips) for j in range(1, chips)]

    def span(k):
        return pl.ds(pl.multiple_of(k * r, r), r)

    own = pl.ds(dp * blocks, blocks)
    ctx_load = pltpu.make_async_copy(context, rows_all.at[own], ctx_sem)
    ctx_load.start()

    def group(n):
        return pl.ds(n * tile, tile)

    def w_load(n):
        at = group(n)
        return pltpu.make_async_copy(weight.at[:, at], held_w.at[:, at], w_sem.at[n])

    for n in range(tiles):
        w_load(n).start()
    res_load = pltpu.make_async_copy(residual, held_res, res_sem)
    res_load.start()

    barrier = pltpu.get_barrier_semaphore()
    for d in dp_at:
        pl.semaphore_signal(barrier, inc=1, device_id={"dp": d}, device_id_type=MESH)
    pl.semaphore_signal(barrier, inc=1, device_id={"tensor": sibling}, device_id_type=MESH)
    for q in chip_at:
        pl.semaphore_signal(barrier, inc=1, device_id={"tensor": q * 2 + core}, device_id_type=MESH)

    @pl.when(sec > 0)
    def _():
        pl.semaphore_signal(barrier, inc=1, device_id={"section": sec - 1}, device_id_type=MESH)

    @pl.when(sec < sections - 1)
    def _():
        pl.semaphore_signal(barrier, inc=1, device_id={"section": sec + 1}, device_id_type=MESH)

    inner = (sec > 0) & (sec < sections - 1)

    @pl.when(inner)
    def _():
        pl.semaphore_wait(barrier, dps + chips + 1)

    @pl.when(jnp.logical_not(inner))
    def _():
        pl.semaphore_wait(barrier, dps + chips)

    def y_copy(k, j):
        return pltpu.make_async_remote_copy(
            src_ref=context.at[:, :, span(k), :],
            dst_ref=rows_all.at[own, :, span(k), :],
            send_sem=y_send.at[k, j],
            recv_sem=y_recv.at[k, j],
            device_id={"dp": dp_at[j]},
            device_id_type=MESH,
        )

    def pair_copy(k, n):
        return pltpu.make_async_remote_copy(
            src_ref=pair_out.at[k, :, :, group(n)],
            dst_ref=pair_in.at[k, :, :, group(n)],
            send_sem=pair_send.at[k, n],
            recv_sem=pair_recv.at[k, n],
            device_id={"tensor": sibling},
            device_id_type=MESH,
        )

    def chip_copy(k, n, j):
        return pltpu.make_async_remote_copy(
            src_ref=chip_out.at[j, span(k), group(n)],
            dst_ref=chip_in.at[j, span(k), group(n)],
            send_sem=chip_send.at[k, n, j],
            recv_sem=chip_recv.at[k, n, j],
            device_id={"tensor": chip_at[j] * 2 + core},
            device_id_type=MESH,
        )

    def z_copy(k, n):
        return pltpu.make_async_remote_copy(
            src_ref=passed.at[span(k), group(n)],
            dst_ref=handoff.at[span(k), group(n)],
            send_sem=z_send.at[k, n],
            recv_sem=z_recv.at[k, n],
            device_id={"section": lax.rem(sec + 1, sections)},
            device_id_type=MESH,
        )

    def sq_copy(k, j):
        return pltpu.make_async_remote_copy(
            src_ref=sq_out.at[k],
            dst_ref=sq_in.at[j, k],
            send_sem=sq_send.at[k, j],
            recv_sem=sq_recv.at[k, j],
            device_id={"dp": dp_at[j]},
            device_id_type=MESH,
        )

    def y_start(k):
        for j in range(dps - 1):
            y_copy(k, j).start()

    y_start(0)

    for j in range(dps - 1):
        y_copy(0, j).wait_send()
    if steps > 1:
        y_start(1)
    ctx_load.wait()

    @pl.when(sec == 0)
    def _():
        def clear(k, carry):
            handoff[span(k), :] = jnp.zeros((r, cols), handoff.dtype)
            return carry

        lax.fori_loop(0, steps, clear, 0)

    def gather(k):
        for j in range(dps - 1):
            y_copy(k, j).wait_recv()

        for q in range(chips):
            lhs[pl.ds(q * r, r), :] = rows_all[q, 1 - core, span(k), :]
            lhs[pl.ds(half + q * r, r), :] = rows_all[q, core, span(k), :]

    def product(k, n):
        @pl.when(k == 0)
        def _():
            w_load(n).wait()

        part = jnp.dot(lhs[...], held_w[:, group(n)], preferred_element_type=jnp.float32)
        pair_out[k, :, :, group(n)] = part[:half].astype(jnp.bfloat16).reshape(chips, r, tile)
        mine[:, :, group(n)] = part[half:].reshape(chips, r, tile)
        pair_copy(k, n).start()

    def combine(k, n):
        pair_copy(k, n).wait_recv()

        def pair_sum(q):
            return mine[q, :, group(n)] + pair_in[k, q, :, group(n)].astype(jnp.float32)

        for j in range(chips - 1):
            chip_out[j, span(k), group(n)] = pair_sum(chip_at[j]).astype(jnp.bfloat16)
            chip_copy(k, n, j).start()
        hidden[span(k), group(n)] = pair_sum(chip)

    def row_mask(k):
        ids = tensor * rows + k * r + lax.broadcasted_iota(jnp.int32, (r, 1), 0)
        return ids < valid_ref[0]

    def add_residual(k, n):
        if n == 0:

            @pl.when(k == 0)
            def _():
                res_load.wait()

        at = group(n)
        for j in range(chips - 1):
            chip_copy(k, n, j).wait_recv()
        h = hidden[span(k), at]
        for j in range(chips - 1):
            h = h + chip_in[j, span(k), at].astype(jnp.float32)
        h = h + held_res[span(k), at].astype(jnp.float32)
        hidden[span(k), at] = h
        passed[span(k), at] = jnp.where(row_mask(k), h, 0.0).astype(jnp.bfloat16)

        @pl.when(sec < sections - 1)
        def _():
            z_copy(k, n).start()

        sq = h * h
        total = sq[:, :128]
        for c in range(1, tile // 128):
            total = total + sq[:, c * 128 : (c + 1) * 128]
        sq_out[k] = total if n == 0 else sq_out[k] + total
        if n == tiles - 1:
            for j in range(dps - 1):
                sq_copy(k, j).start()

    def normalize(k):
        total = sq_out[k]
        for j in range(dps - 1):
            sq_copy(k, j).wait_recv()
            total = total + sq_in[j, k]
        mean_sq = jnp.sum(total, axis=1, keepdims=True) / (dps * cols)
        scale = jnp.where(row_mask(k), lax.rsqrt(mean_sq + 1e-06), 0.0)
        for n in range(tiles):
            at = pl.ds(n * tile, tile)
            g = gain[:, pl.ds(pl.multiple_of(dp * cols + n * tile, tile), tile)]
            normed[span(k), at] = (hidden[span(k), at] * scale * g).astype(jnp.bfloat16)

    def step(s, carry):
        @pl.when(s < steps)
        def _():
            gather(s)

        for n in range(tiles):

            @pl.when(s < steps)
            def _():
                product(s, n)
                if n > 0:
                    combine(s, n - 1)

            if n == max(0, tiles - 2):

                @pl.when(s + 2 < steps)
                def _():
                    y_start(s + 2)

            if n + first < tiles:

                @pl.when((s > 0) & (s <= steps))
                def _():
                    add_residual(s - 1, n + first)

        @pl.when(s < steps)
        def _():
            combine(s, tiles - 1)
            for n in range(first):
                add_residual(s, n)

        @pl.when(s > 1)
        def _():
            normalize(s - 2)

        return carry

    lax.fori_loop(0, steps + 2, step, 0)

    def drain(k, carry):
        @pl.when(k > 0)
        def _():
            for j in range(dps - 1):
                y_copy(k, j).wait_send()

        for j in range(dps - 1):
            sq_copy(k, j).wait_send()
        for n in range(tiles):
            pair_copy(k, n).wait_send()
            for j in range(chips - 1):
                chip_copy(k, n, j).wait_send()

        @pl.when(sec < sections - 1)
        def _():
            for n in range(tiles):
                z_copy(k, n).wait_send()

        @pl.when(sec > 0)
        def _():
            for n in range(tiles):
                z_copy(k, n).wait_recv()

        return carry

    lax.fori_loop(0, steps, drain, 0)


def on_device(context, residual, out_weight, norm_gain, valid_tokens):
    sections, dps, tensors = (lax.axis_size(a) for a in ("section", "dp", "tensor"))
    chips = tensors // 2
    rows, cols = residual.shape[1:]
    local, depth = context.shape[1:]
    blocks = local // (2 * rows)
    assert blocks * dps == chips
    r = max(16, rows // PIECES)
    steps = rows // r
    tile = cols // GROUPS
    tiles = GROUPS
    sizes = (sections, dps, chips, blocks, rows, depth, cols, r, steps, tile)
    bf16, f32 = jnp.bfloat16, jnp.float32
    dma = pltpu.SemaphoreType.DMA
    total_rows = local * dps
    anywhere = pl.BlockSpec(memory_space=pl.ANY)
    out = pltpu.VMEM((rows, cols), bf16)
    normed, handoff = pl.pallas_call(
        functools.partial(relay_kernel, sizes),
        out_shape=(out, out),
        in_specs=[
            pl.BlockSpec(memory_space=pltpu.SMEM),
            anywhere,
            anywhere,
            anywhere,
            pl.BlockSpec(memory_space=pltpu.VMEM),
        ],
        out_specs=(pl.BlockSpec(memory_space=pltpu.VMEM),) * 2,
        scratch_shapes=[
            pltpu.VMEM((chips, 2, rows, depth), bf16),
            pltpu.VMEM((2 * chips * r, depth), bf16),
            pltpu.VMEM((depth, cols), bf16),
            pltpu.VMEM((rows, cols), bf16),
            pltpu.VMEM((chips, r, cols), f32),
            pltpu.VMEM((steps, chips, r, cols), bf16),
            pltpu.VMEM((steps, chips, r, cols), bf16),
            pltpu.VMEM((chips - 1, rows, cols), bf16),
            pltpu.VMEM((chips - 1, rows, cols), bf16),
            pltpu.VMEM((rows, cols), f32),
            pltpu.VMEM((rows, cols), bf16),
            pltpu.VMEM((steps, r, 128), f32),
            pltpu.VMEM((dps - 1, steps, r, 128), f32),
            dma,
            dma((tiles,)),
            dma,
            dma((steps, dps - 1)),
            dma((steps, dps - 1)),
            dma((steps, tiles)),
            dma((steps, tiles)),
            dma((steps, tiles, chips - 1)),
            dma((steps, tiles, chips - 1)),
            dma((steps, tiles)),
            dma((steps, tiles)),
            dma((steps, dps - 1)),
            dma((steps, dps - 1)),
        ],
        compiler_params=pltpu.CompilerParams(
            collective_id=0, has_side_effects=True, vmem_limit_bytes=56 * 2**20
        ),
        cost_estimate=pl.CostEstimate(
            flops=2 * total_rows * depth * cols,
            bytes_accessed=2 * (depth * cols + local * depth + 3 * rows * cols),
            transcendentals=0,
        ),
        name="relay",
    )(
        valid_tokens,
        context.reshape(blocks, 2, rows, depth),
        residual[0],
        out_weight[0],
        norm_gain,
    )
    return (normed[None], handoff[None])


def solution(mesh):
    placed = (
        P("section", "dp", "tensor"),
        P("section", "tensor", "dp"),
        P("section", "tensor", "dp"),
        P("section", None),
        P("section"),
    )
    return jax.shard_map(
        on_device,
        mesh=mesh,
        in_specs=placed,
        out_specs=(P("section", "tensor", "dp"), P("section", "tensor", "dp")),
        check_vma=False,
    )
```

```python
import functools

import jax
import jax.numpy as jnp
from jax import lax
from jax.experimental import pallas as pl
from jax.experimental.pallas import tpu as pltpu
from jax.sharding import PartitionSpec as P

MESH = pl.DeviceIdType.MESH
PIECES = 8
GROUPS = 4


def relay_kernel(
    sizes, valid_ref, context, residual, weight, gain, normed, handoff,
    rows_all, lhs, held_w, held_res, mine, pair_out, pair_in, chip_out, chip_in,
    hidden, passed, sq_out, sq_in,
    ctx_sem, w_sem, res_sem, y_send, y_recv, pair_send, pair_recv,
    chip_send, chip_recv, z_send, z_recv, sq_send, sq_recv,
):
    sections, dps, chips, blocks, rows, depth, cols, r, steps, tile = sizes
    tiles = cols // tile
    half = chips * r
    sec = lax.axis_index("section")
    dp = lax.axis_index("dp")
    tensor = lax.axis_index("tensor")
    core = lax.rem(tensor, 2)
    chip = lax.div(tensor, 2)
    sibling = tensor + 1 - 2 * core
    dp_at = [lax.rem(dp + j, dps) for j in range(1, dps)]
    chip_at = [lax.rem(chip + j, chips) for j in range(1, chips)]

    def span(k):
        return pl.ds(pl.multiple_of(k * r, r), r)

    own = pl.ds(dp * blocks, blocks)
    ctx_load = pltpu.make_async_copy(context, rows_all.at[own], ctx_sem)
    ctx_load.start()

    def group(n):
        return pl.ds(n * tile, tile)

    def w_load(n):
        at = group(n)
        return pltpu.make_async_copy(weight.at[:, at], held_w.at[:, at], w_sem.at[n])

    for n in range(tiles):
        w_load(n).start()
    res_load = pltpu.make_async_copy(residual, held_res, res_sem)
    res_load.start()

    barrier = pltpu.get_barrier_semaphore()
    for d in dp_at:
        pl.semaphore_signal(barrier, inc=1, device_id={"dp": d}, device_id_type=MESH)
    pl.semaphore_signal(barrier, inc=1, device_id={"tensor": sibling}, device_id_type=MESH)
    for q in chip_at:
        pl.semaphore_signal(barrier, inc=1, device_id={"tensor": q * 2 + core}, device_id_type=MESH)

    @pl.when(sec > 0)
    def _():
        pl.semaphore_signal(barrier, inc=1, device_id={"section": sec - 1}, device_id_type=MESH)

    @pl.when(sec < sections - 1)
    def _():
        pl.semaphore_signal(barrier, inc=1, device_id={"section": sec + 1}, device_id_type=MESH)

    inner = (sec > 0) & (sec < sections - 1)

    @pl.when(inner)
    def _():
        pl.semaphore_wait(barrier, dps + chips + 1)

    @pl.when(jnp.logical_not(inner))
    def _():
        pl.semaphore_wait(barrier, dps + chips)

    def y_copy(k, j):
        return pltpu.make_async_remote_copy(
            src_ref=context.at[:, :, span(k), :],
            dst_ref=rows_all.at[own, :, span(k), :],
            send_sem=y_send.at[k, j],
            recv_sem=y_recv.at[k, j],
            device_id={"dp": dp_at[j]},
            device_id_type=MESH,
        )

    def pair_copy(k, n):
        return pltpu.make_async_remote_copy(
            src_ref=pair_out.at[k, :, :, group(n)],
            dst_ref=pair_in.at[k, :, :, group(n)],
            send_sem=pair_send.at[k, n],
            recv_sem=pair_recv.at[k, n],
            device_id={"tensor": sibling},
            device_id_type=MESH,
        )

    def chip_copy(k, n, j):
        return pltpu.make_async_remote_copy(
            src_ref=chip_out.at[j, span(k), group(n)],
            dst_ref=chip_in.at[j, span(k), group(n)],
            send_sem=chip_send.at[k, n, j],
            recv_sem=chip_recv.at[k, n, j],
            device_id={"tensor": chip_at[j] * 2 + core},
            device_id_type=MESH,
        )

    def z_copy(k, n):
        return pltpu.make_async_remote_copy(
            src_ref=passed.at[span(k), group(n)],
            dst_ref=handoff.at[span(k), group(n)],
            send_sem=z_send.at[k, n],
            recv_sem=z_recv.at[k, n],
            device_id={"section": lax.rem(sec + 1, sections)},
            device_id_type=MESH,
        )

    def sq_copy(k, j):
        return pltpu.make_async_remote_copy(
            src_ref=sq_out.at[k],
            dst_ref=sq_in.at[j, k],
            send_sem=sq_send.at[k, j],
            recv_sem=sq_recv.at[k, j],
            device_id={"dp": dp_at[j]},
            device_id_type=MESH,
        )

    def y_start(k):
        for j in range(dps - 1):
            y_copy(k, j).start()

    y_start(0)

    for j in range(dps - 1):
        y_copy(0, j).wait_send()
    if steps > 1:
        y_start(1)
    ctx_load.wait()

    @pl.when(sec == 0)
    def _():
        def clear(k, carry):
            handoff[span(k), :] = jnp.zeros((r, cols), handoff.dtype)
            return carry

        lax.fori_loop(0, steps, clear, 0)

    def gather(k):
        for j in range(dps - 1):
            y_copy(k, j).wait_recv()

        for q in range(chips):
            lhs[pl.ds(q * r, r), :] = rows_all[q, 1 - core, span(k), :]
            lhs[pl.ds(half + q * r, r), :] = rows_all[q, core, span(k), :]

    def product(k, n):
        @pl.when(k == 0)
        def _():
            w_load(n).wait()

        part = jnp.dot(lhs[...], held_w[:, group(n)], preferred_element_type=jnp.float32)
        pair_out[k, :, :, group(n)] = part[:half].astype(jnp.bfloat16).reshape(chips, r, tile)
        mine[:, :, group(n)] = part[half:].reshape(chips, r, tile)
        pair_copy(k, n).start()

    def combine(k, n):
        pair_copy(k, n).wait_recv()

        def pair_sum(q):
            return mine[q, :, group(n)] + pair_in[k, q, :, group(n)].astype(jnp.float32)

        for j in range(chips - 1):
            chip_out[j, span(k), group(n)] = pair_sum(chip_at[j]).astype(jnp.bfloat16)
            chip_copy(k, n, j).start()
        hidden[span(k), group(n)] = pair_sum(chip)

    def row_mask(k):
        ids = tensor * rows + k * r + lax.broadcasted_iota(jnp.int32, (r, 1), 0)
        return ids < valid_ref[0]

    def add_residual(k, n):
        if n == 0:

            @pl.when(k == 0)
            def _():
                res_load.wait()

        at = group(n)
        for j in range(chips - 1):
            chip_copy(k, n, j).wait_recv()
        h = hidden[span(k), at]
        for j in range(chips - 1):
            h = h + chip_in[j, span(k), at].astype(jnp.float32)
        h = h + held_res[span(k), at].astype(jnp.float32)
        hidden[span(k), at] = h
        passed[span(k), at] = jnp.where(row_mask(k), h, 0.0).astype(jnp.bfloat16)

        @pl.when(sec < sections - 1)
        def _():
            z_copy(k, n).start()

        sq = h * h
        total = sq[:, :128]
        for c in range(1, tile // 128):
            total = total + sq[:, c * 128 : (c + 1) * 128]
        sq_out[k] = total if n == 0 else sq_out[k] + total
        if n == tiles - 1:
            for j in range(dps - 1):
                sq_copy(k, j).start()

    def normalize(k):
        total = sq_out[k]
        for j in range(dps - 1):
            sq_copy(k, j).wait_recv()
            total = total + sq_in[j, k]
        mean_sq = jnp.sum(total, axis=1, keepdims=True) / (dps * cols)
        scale = jnp.where(row_mask(k), lax.rsqrt(mean_sq + 1e-06), 0.0)
        for n in range(tiles):
            at = pl.ds(n * tile, tile)
            g = gain[:, pl.ds(pl.multiple_of(dp * cols + n * tile, tile), tile)]
            normed[span(k), at] = (hidden[span(k), at] * scale * g).astype(jnp.bfloat16)

    def step(s, carry):
        @pl.when(s < steps)
        def _():
            gather(s)

        for n in range(tiles):

            @pl.when(s < steps)
            def _():
                product(s, n)
                if n > 0:
                    combine(s, n - 1)

            if n == 0:

                @pl.when((s > 0) & (s <= steps))
                def _():
                    combine(s - 1, tiles - 1)

            if n == max(0, tiles - 2):

                @pl.when(s + 2 < steps)
                def _():
                    y_start(s + 2)

            @pl.when((s > 0) & (s <= steps))
            def _():
                add_residual(s - 1, n)

        @pl.when(s > 1)
        def _():
            normalize(s - 2)

        return carry

    lax.fori_loop(0, steps + 2, step, 0)

    def drain(k, carry):
        @pl.when(k > 0)
        def _():
            for j in range(dps - 1):
                y_copy(k, j).wait_send()

        for j in range(dps - 1):
            sq_copy(k, j).wait_send()
        for n in range(tiles):
            pair_copy(k, n).wait_send()
            for j in range(chips - 1):
                chip_copy(k, n, j).wait_send()

        @pl.when(sec < sections - 1)
        def _():
            for n in range(tiles):
                z_copy(k, n).wait_send()

        @pl.when(sec > 0)
        def _():
            for n in range(tiles):
                z_copy(k, n).wait_recv()

        return carry

    lax.fori_loop(0, steps, drain, 0)


def on_device(context, residual, out_weight, norm_gain, valid_tokens):
    sections, dps, tensors = (lax.axis_size(a) for a in ("section", "dp", "tensor"))
    chips = tensors // 2
    rows, cols = residual.shape[1:]
    local, depth = context.shape[1:]
    blocks = local // (2 * rows)
    assert blocks * dps == chips
    r = max(16, rows // PIECES)
    steps = rows // r
    tile = cols // GROUPS
    tiles = GROUPS
    sizes = (sections, dps, chips, blocks, rows, depth, cols, r, steps, tile)
    bf16, f32 = jnp.bfloat16, jnp.float32
    dma = pltpu.SemaphoreType.DMA
    total_rows = local * dps
    anywhere = pl.BlockSpec(memory_space=pl.ANY)
    out = pltpu.VMEM((rows, cols), bf16)
    normed, handoff = pl.pallas_call(
        functools.partial(relay_kernel, sizes),
        out_shape=(out, out),
        in_specs=[
            pl.BlockSpec(memory_space=pltpu.SMEM),
            anywhere,
            anywhere,
            anywhere,
            pl.BlockSpec(memory_space=pltpu.VMEM),
        ],
        out_specs=(pl.BlockSpec(memory_space=pltpu.VMEM),) * 2,
        scratch_shapes=[
            pltpu.VMEM((chips, 2, rows, depth), bf16),
            pltpu.VMEM((2 * chips * r, depth), bf16),
            pltpu.VMEM((depth, cols), bf16),
            pltpu.VMEM((rows, cols), bf16),
            pltpu.VMEM((chips, r, cols), f32),
            pltpu.VMEM((steps, chips, r, cols), bf16),
            pltpu.VMEM((steps, chips, r, cols), bf16),
            pltpu.VMEM((chips - 1, rows, cols), bf16),
            pltpu.VMEM((chips - 1, rows, cols), bf16),
            pltpu.VMEM((rows, cols), f32),
            pltpu.VMEM((rows, cols), bf16),
            pltpu.VMEM((steps, r, 128), f32),
            pltpu.VMEM((dps - 1, steps, r, 128), f32),
            dma,
            dma((tiles,)),
            dma,
            dma((steps, dps - 1)),
            dma((steps, dps - 1)),
            dma((steps, tiles)),
            dma((steps, tiles)),
            dma((steps, tiles, chips - 1)),
            dma((steps, tiles, chips - 1)),
            dma((steps, tiles)),
            dma((steps, tiles)),
            dma((steps, dps - 1)),
            dma((steps, dps - 1)),
        ],
        compiler_params=pltpu.CompilerParams(
            collective_id=0, has_side_effects=True, vmem_limit_bytes=56 * 2**20
        ),
        cost_estimate=pl.CostEstimate(
            flops=2 * total_rows * depth * cols,
            bytes_accessed=2 * (depth * cols + local * depth + 3 * rows * cols),
            transcendentals=0,
        ),
        name="relay",
    )(
        valid_tokens,
        context.reshape(blocks, 2, rows, depth),
        residual[0],
        out_weight[0],
        norm_gain,
    )
    return (normed[None], handoff[None])


def solution(mesh):
    placed = (
        P("section", "dp", "tensor"),
        P("section", "tensor", "dp"),
        P("section", "tensor", "dp"),
        P("section", None),
        P("section"),
    )
    return jax.shard_map(
        on_device,
        mesh=mesh,
        in_specs=placed,
        out_specs=(P("section", "tensor", "dp"), P("section", "tensor", "dp")),
        check_vma=False,
    )
```

```python
import functools

import jax
import jax.numpy as jnp
from jax import lax
from jax.experimental import pallas as pl
from jax.experimental.pallas import tpu as pltpu
from jax.sharding import PartitionSpec as P

MESH = pl.DeviceIdType.MESH
PIECES = 16
GROUPS = 2


def relay_kernel(
    sizes, valid_ref, context, residual, weight, gain, normed, handoff,
    rows_all, lhs, held_w, held_res, mine, pair_out, pair_in, chip_out, chip_in,
    hidden, passed, sq_out, sq_in,
    ctx_sem, w_sem, res_sem, y_send, y_recv, pair_send, pair_recv,
    chip_send, chip_recv, z_send, z_recv, sq_send, sq_recv,
):
    sections, dps, chips, blocks, rows, depth, cols, r, steps, tile = sizes
    tiles = cols // tile
    half = chips * r
    sec = lax.axis_index("section")
    dp = lax.axis_index("dp")
    tensor = lax.axis_index("tensor")
    core = lax.rem(tensor, 2)
    chip = lax.div(tensor, 2)
    sibling = tensor + 1 - 2 * core
    dp_at = [lax.rem(dp + j, dps) for j in range(1, dps)]
    chip_at = [lax.rem(chip + j, chips) for j in range(1, chips)]

    def span(k):
        return pl.ds(pl.multiple_of(k * r, r), r)

    own = pl.ds(dp * blocks, blocks)
    ctx_load = pltpu.make_async_copy(context, rows_all.at[own], ctx_sem)
    ctx_load.start()

    def group(n):
        return pl.ds(n * tile, tile)

    def w_load(n):
        at = group(n)
        return pltpu.make_async_copy(weight.at[:, at], held_w.at[:, at], w_sem.at[n])

    for n in range(tiles):
        w_load(n).start()
    res_load = pltpu.make_async_copy(residual, held_res, res_sem)
    res_load.start()

    barrier = pltpu.get_barrier_semaphore()
    for d in dp_at:
        pl.semaphore_signal(barrier, inc=1, device_id={"dp": d}, device_id_type=MESH)
    pl.semaphore_signal(barrier, inc=1, device_id={"tensor": sibling}, device_id_type=MESH)
    for q in chip_at:
        pl.semaphore_signal(barrier, inc=1, device_id={"tensor": q * 2 + core}, device_id_type=MESH)

    @pl.when(sec > 0)
    def _():
        pl.semaphore_signal(barrier, inc=1, device_id={"section": sec - 1}, device_id_type=MESH)

    @pl.when(sec < sections - 1)
    def _():
        pl.semaphore_signal(barrier, inc=1, device_id={"section": sec + 1}, device_id_type=MESH)

    inner = (sec > 0) & (sec < sections - 1)

    @pl.when(inner)
    def _():
        pl.semaphore_wait(barrier, dps + chips + 1)

    @pl.when(jnp.logical_not(inner))
    def _():
        pl.semaphore_wait(barrier, dps + chips)

    def y_copy(k, j):
        return pltpu.make_async_remote_copy(
            src_ref=context.at[:, :, span(k), :],
            dst_ref=rows_all.at[own, :, span(k), :],
            send_sem=y_send.at[k, j],
            recv_sem=y_recv.at[k, j],
            device_id={"dp": dp_at[j]},
            device_id_type=MESH,
        )

    def pair_copy(k, n):
        return pltpu.make_async_remote_copy(
            src_ref=pair_out.at[k, :, :, group(n)],
            dst_ref=pair_in.at[k, :, :, group(n)],
            send_sem=pair_send.at[k, n],
            recv_sem=pair_recv.at[k, n],
            device_id={"tensor": sibling},
            device_id_type=MESH,
        )

    def chip_copy(k, n, j):
        return pltpu.make_async_remote_copy(
            src_ref=chip_out.at[j, span(k), group(n)],
            dst_ref=chip_in.at[j, span(k), group(n)],
            send_sem=chip_send.at[k, n, j],
            recv_sem=chip_recv.at[k, n, j],
            device_id={"tensor": chip_at[j] * 2 + core},
            device_id_type=MESH,
        )

    def z_copy(k, n):
        return pltpu.make_async_remote_copy(
            src_ref=passed.at[span(k), group(n)],
            dst_ref=handoff.at[span(k), group(n)],
            send_sem=z_send.at[k, n],
            recv_sem=z_recv.at[k, n],
            device_id={"section": lax.rem(sec + 1, sections)},
            device_id_type=MESH,
        )

    def sq_copy(k, j):
        return pltpu.make_async_remote_copy(
            src_ref=sq_out.at[k],
            dst_ref=sq_in.at[j, k],
            send_sem=sq_send.at[k, j],
            recv_sem=sq_recv.at[k, j],
            device_id={"dp": dp_at[j]},
            device_id_type=MESH,
        )

    def y_start(k):
        for j in range(dps - 1):
            y_copy(k, j).start()

    y_start(0)

    for j in range(dps - 1):
        y_copy(0, j).wait_send()
    if steps > 1:
        y_start(1)
    ctx_load.wait()

    @pl.when(sec == 0)
    def _():
        def clear(k, carry):
            handoff[span(k), :] = jnp.zeros((r, cols), handoff.dtype)
            return carry

        lax.fori_loop(0, steps, clear, 0)

    def gather(k):
        for j in range(dps - 1):
            y_copy(k, j).wait_recv()

        @pl.when(k + 2 < steps)
        def _():
            y_start(k + 2)

        for q in range(chips):
            lhs[pl.ds(q * r, r), :] = rows_all[q, 1 - core, span(k), :]
            lhs[pl.ds(half + q * r, r), :] = rows_all[q, core, span(k), :]

    def product(k, n):
        @pl.when(k == 0)
        def _():
            w_load(n).wait()

        part = jnp.dot(lhs[...], held_w[:, group(n)], preferred_element_type=jnp.float32)
        pair_out[k, :, :, group(n)] = part[:half].astype(jnp.bfloat16).reshape(chips, r, tile)
        mine[:, :, group(n)] = part[half:].reshape(chips, r, tile)
        pair_copy(k, n).start()

    def combine(k, n):
        pair_copy(k, n).wait_recv()

        def pair_sum(q):
            return mine[q, :, group(n)] + pair_in[k, q, :, group(n)].astype(jnp.float32)

        for j in range(chips - 1):
            chip_out[j, span(k), group(n)] = pair_sum(chip_at[j]).astype(jnp.bfloat16)
            chip_copy(k, n, j).start()
        hidden[span(k), group(n)] = pair_sum(chip)

    def row_mask(k):
        ids = tensor * rows + k * r + lax.broadcasted_iota(jnp.int32, (r, 1), 0)
        return ids < valid_ref[0]

    def add_residual(k, n):
        if n == 0:

            @pl.when(k == 0)
            def _():
                res_load.wait()

        at = group(n)
        for j in range(chips - 1):
            chip_copy(k, n, j).wait_recv()
        h = hidden[span(k), at]
        for j in range(chips - 1):
            h = h + chip_in[j, span(k), at].astype(jnp.float32)
        h = h + held_res[span(k), at].astype(jnp.float32)
        hidden[span(k), at] = h
        passed[span(k), at] = jnp.where(row_mask(k), h, 0.0).astype(jnp.bfloat16)

        @pl.when(sec < sections - 1)
        def _():
            z_copy(k, n).start()

        sq = h * h
        total = sq[:, :128]
        for c in range(1, tile // 128):
            total = total + sq[:, c * 128 : (c + 1) * 128]
        sq_out[k] = total if n == 0 else sq_out[k] + total
        if n == tiles - 1:
            for j in range(dps - 1):
                sq_copy(k, j).start()

    def normalize(k):
        total = sq_out[k]
        for j in range(dps - 1):
            sq_copy(k, j).wait_recv()
            total = total + sq_in[j, k]
        mean_sq = jnp.sum(total, axis=1, keepdims=True) / (dps * cols)
        scale = jnp.where(row_mask(k), lax.rsqrt(mean_sq + 1e-06), 0.0)
        for n in range(tiles):
            at = pl.ds(n * tile, tile)
            g = gain[:, pl.ds(pl.multiple_of(dp * cols + n * tile, tile), tile)]
            normed[span(k), at] = (hidden[span(k), at] * scale * g).astype(jnp.bfloat16)

    def step(s, carry):
        @pl.when(s < steps)
        def _():
            gather(s)

        for n in range(tiles):

            @pl.when(s < steps)
            def _():
                product(s, n)
                if n > 0:
                    combine(s, n - 1)

            if n == 0:

                @pl.when((s > 0) & (s <= steps))
                def _():
                    combine(s - 1, tiles - 1)

            @pl.when((s > 0) & (s <= steps))
            def _():
                add_residual(s - 1, n)

        @pl.when(s > 1)
        def _():
            normalize(s - 2)

        return carry

    lax.fori_loop(0, steps + 2, step, 0)

    def drain(k, carry):
        @pl.when(k > 0)
        def _():
            for j in range(dps - 1):
                y_copy(k, j).wait_send()

        for j in range(dps - 1):
            sq_copy(k, j).wait_send()
        for n in range(tiles):
            pair_copy(k, n).wait_send()
            for j in range(chips - 1):
                chip_copy(k, n, j).wait_send()

        @pl.when(sec < sections - 1)
        def _():
            for n in range(tiles):
                z_copy(k, n).wait_send()

        @pl.when(sec > 0)
        def _():
            for n in range(tiles):
                z_copy(k, n).wait_recv()

        return carry

    lax.fori_loop(0, steps, drain, 0)


def on_device(context, residual, out_weight, norm_gain, valid_tokens):
    sections, dps, tensors = (lax.axis_size(a) for a in ("section", "dp", "tensor"))
    chips = tensors // 2
    rows, cols = residual.shape[1:]
    local, depth = context.shape[1:]
    blocks = local // (2 * rows)
    assert blocks * dps == chips
    r = max(16, rows // PIECES)
    steps = rows // r
    tile = cols // GROUPS
    tiles = GROUPS
    sizes = (sections, dps, chips, blocks, rows, depth, cols, r, steps, tile)
    bf16, f32 = jnp.bfloat16, jnp.float32
    dma = pltpu.SemaphoreType.DMA
    total_rows = local * dps
    anywhere = pl.BlockSpec(memory_space=pl.ANY)
    out = pltpu.VMEM((rows, cols), bf16)
    normed, handoff = pl.pallas_call(
        functools.partial(relay_kernel, sizes),
        out_shape=(out, out),
        in_specs=[
            pl.BlockSpec(memory_space=pltpu.SMEM),
            anywhere,
            anywhere,
            anywhere,
            pl.BlockSpec(memory_space=pltpu.VMEM),
        ],
        out_specs=(pl.BlockSpec(memory_space=pltpu.VMEM),) * 2,
        scratch_shapes=[
            pltpu.VMEM((chips, 2, rows, depth), bf16),
            pltpu.VMEM((2 * chips * r, depth), bf16),
            pltpu.VMEM((depth, cols), bf16),
            pltpu.VMEM((rows, cols), bf16),
            pltpu.VMEM((chips, r, cols), f32),
            pltpu.VMEM((steps, chips, r, cols), bf16),
            pltpu.VMEM((steps, chips, r, cols), bf16),
            pltpu.VMEM((chips - 1, rows, cols), bf16),
            pltpu.VMEM((chips - 1, rows, cols), bf16),
            pltpu.VMEM((rows, cols), f32),
            pltpu.VMEM((rows, cols), bf16),
            pltpu.VMEM((steps, r, 128), f32),
            pltpu.VMEM((dps - 1, steps, r, 128), f32),
            dma,
            dma((tiles,)),
            dma,
            dma((steps, dps - 1)),
            dma((steps, dps - 1)),
            dma((steps, tiles)),
            dma((steps, tiles)),
            dma((steps, tiles, chips - 1)),
            dma((steps, tiles, chips - 1)),
            dma((steps, tiles)),
            dma((steps, tiles)),
            dma((steps, dps - 1)),
            dma((steps, dps - 1)),
        ],
        compiler_params=pltpu.CompilerParams(
            collective_id=0, has_side_effects=True, vmem_limit_bytes=56 * 2**20
        ),
        cost_estimate=pl.CostEstimate(
            flops=2 * total_rows * depth * cols,
            bytes_accessed=2 * (depth * cols + local * depth + 3 * rows * cols),
            transcendentals=0,
        ),
        name="relay",
    )(
        valid_tokens,
        context.reshape(blocks, 2, rows, depth),
        residual[0],
        out_weight[0],
        norm_gain,
    )
    return (normed[None], handoff[None])


def solution(mesh):
    placed = (
        P("section", "dp", "tensor"),
        P("section", "tensor", "dp"),
        P("section", "tensor", "dp"),
        P("section", None),
        P("section"),
    )
    return jax.shard_map(
        on_device,
        mesh=mesh,
        in_specs=placed,
        out_specs=(P("section", "tensor", "dp"), P("section", "tensor", "dp")),
        check_vma=False,
    )
```

```python
import functools

import jax
import jax.numpy as jnp
from jax import lax
from jax.experimental import pallas as pl
from jax.experimental.pallas import tpu as pltpu
from jax.sharding import PartitionSpec as P

MESH = pl.DeviceIdType.MESH
PIECES = 8
GROUPS = 4


def relay_kernel(
    sizes, valid_ref, context, residual, weight, gain, normed, handoff,
    rows_all, lhs, held_w, held_res, mine, pair_out, pair_in, chip_out, chip_in,
    hidden, passed, sq_out, sq_in,
    ctx_sem, w_sem, res_sem, y_send, y_recv, pair_send, pair_recv,
    chip_send, chip_recv, z_send, z_recv, sq_send, sq_recv,
):
    sections, dps, chips, blocks, rows, depth, cols, r, steps, tile = sizes
    tiles = cols // tile
    half = chips * r
    sec = lax.axis_index("section")
    dp = lax.axis_index("dp")
    tensor = lax.axis_index("tensor")
    core = lax.rem(tensor, 2)
    chip = lax.div(tensor, 2)
    sibling = tensor + 1 - 2 * core
    dp_at = [lax.rem(dp + j, dps) for j in range(1, dps)]
    chip_at = [lax.rem(chip + j, chips) for j in range(1, chips)]

    def span(k):
        return pl.ds(pl.multiple_of(k * r, r), r)

    own = pl.ds(dp * blocks, blocks)
    ctx_load = pltpu.make_async_copy(context, rows_all.at[own], ctx_sem)
    ctx_load.start()

    def group(n):
        return pl.ds(n * tile, tile)

    def w_load(n):
        at = group(n)
        return pltpu.make_async_copy(weight.at[:, at], held_w.at[:, at], w_sem.at[n])

    for n in range(tiles):
        w_load(n).start()
    res_load = pltpu.make_async_copy(residual, held_res, res_sem)
    res_load.start()

    barrier = pltpu.get_barrier_semaphore()
    for d in dp_at:
        pl.semaphore_signal(barrier, inc=1, device_id={"dp": d}, device_id_type=MESH)
    pl.semaphore_signal(barrier, inc=1, device_id={"tensor": sibling}, device_id_type=MESH)
    for q in chip_at:
        pl.semaphore_signal(barrier, inc=1, device_id={"tensor": q * 2 + core}, device_id_type=MESH)

    @pl.when(sec > 0)
    def _():
        pl.semaphore_signal(barrier, inc=1, device_id={"section": sec - 1}, device_id_type=MESH)

    @pl.when(sec < sections - 1)
    def _():
        pl.semaphore_signal(barrier, inc=1, device_id={"section": sec + 1}, device_id_type=MESH)

    inner = (sec > 0) & (sec < sections - 1)

    @pl.when(inner)
    def _():
        pl.semaphore_wait(barrier, dps + chips + 1)

    @pl.when(jnp.logical_not(inner))
    def _():
        pl.semaphore_wait(barrier, dps + chips)

    def y_copy(k, j):
        return pltpu.make_async_remote_copy(
            src_ref=context.at[:, :, span(k), :],
            dst_ref=rows_all.at[own, :, span(k), :],
            send_sem=y_send.at[k, j],
            recv_sem=y_recv.at[k, j],
            device_id={"dp": dp_at[j]},
            device_id_type=MESH,
        )

    def pair_copy(k, n):
        return pltpu.make_async_remote_copy(
            src_ref=pair_out.at[k, :, :, group(n)],
            dst_ref=pair_in.at[k, :, :, group(n)],
            send_sem=pair_send.at[k, n],
            recv_sem=pair_recv.at[k, n],
            device_id={"tensor": sibling},
            device_id_type=MESH,
        )

    def chip_copy(k, n, j):
        return pltpu.make_async_remote_copy(
            src_ref=chip_out.at[j, span(k), group(n)],
            dst_ref=chip_in.at[j, span(k), group(n)],
            send_sem=chip_send.at[k, n, j],
            recv_sem=chip_recv.at[k, n, j],
            device_id={"tensor": chip_at[j] * 2 + core},
            device_id_type=MESH,
        )

    def z_copy(k, n):
        return pltpu.make_async_remote_copy(
            src_ref=passed.at[span(k), group(n)],
            dst_ref=handoff.at[span(k), group(n)],
            send_sem=z_send.at[k, n],
            recv_sem=z_recv.at[k, n],
            device_id={"section": lax.rem(sec + 1, sections)},
            device_id_type=MESH,
        )

    def sq_copy(k, j):
        return pltpu.make_async_remote_copy(
            src_ref=sq_out.at[k],
            dst_ref=sq_in.at[j, k],
            send_sem=sq_send.at[k, j],
            recv_sem=sq_recv.at[k, j],
            device_id={"dp": dp_at[j]},
            device_id_type=MESH,
        )

    def y_start(k):
        for j in range(dps - 1):
            y_copy(k, j).start()

    y_start(0)

    for j in range(dps - 1):
        y_copy(0, j).wait_send()
    if steps > 1:
        y_start(1)
    ctx_load.wait()

    @pl.when(sec == 0)
    def _():
        def clear(k, carry):
            handoff[span(k), :] = jnp.zeros((r, cols), handoff.dtype)
            return carry

        lax.fori_loop(0, steps, clear, 0)

    def gather(k):
        for j in range(dps - 1):
            y_copy(k, j).wait_recv()

        @pl.when(k + 2 < steps)
        def _():
            y_start(k + 2)

        for q in range(chips):
            lhs[pl.ds(q * r, r), :] = rows_all[q, 1 - core, span(k), :]
            lhs[pl.ds(half + q * r, r), :] = rows_all[q, core, span(k), :]

    def product(k, n):
        @pl.when(k == 0)
        def _():
            w_load(n).wait()

        part = jnp.dot(lhs[...], held_w[:, group(n)], preferred_element_type=jnp.float32)
        pair_out[k, :, :, group(n)] = part[:half].astype(jnp.bfloat16).reshape(chips, r, tile)
        mine[:, :, group(n)] = part[half:].reshape(chips, r, tile)
        pair_copy(k, n).start()

    def combine(k, n):
        pair_copy(k, n).wait_recv()

        def pair_sum(q):
            return mine[q, :, group(n)] + pair_in[k, q, :, group(n)].astype(jnp.float32)

        for j in range(chips - 1):
            chip_out[j, span(k), group(n)] = pair_sum(chip_at[j]).astype(jnp.bfloat16)
            chip_copy(k, n, j).start()
        hidden[span(k), group(n)] = pair_sum(chip)

    def row_mask(k):
        ids = tensor * rows + k * r + lax.broadcasted_iota(jnp.int32, (r, 1), 0)
        return ids < valid_ref[0]

    def add_residual(k, n):
        if n == 0:

            @pl.when(k == 0)
            def _():
                res_load.wait()

        at = group(n)
        for j in range(chips - 1):
            chip_copy(k, n, j).wait_recv()
        h = hidden[span(k), at]
        for j in range(chips - 1):
            h = h + chip_in[j, span(k), at].astype(jnp.float32)
        h = h + held_res[span(k), at].astype(jnp.float32)
        hidden[span(k), at] = h
        passed[span(k), at] = jnp.where(row_mask(k), h, 0.0).astype(jnp.bfloat16)

        @pl.when(sec < sections - 1)
        def _():
            z_copy(k, n).start()

        sq = h * h
        total = sq[:, :128]
        for c in range(1, tile // 128):
            total = total + sq[:, c * 128 : (c + 1) * 128]
        sq_out[k] = total if n == 0 else sq_out[k] + total
        if n == tiles - 1:
            for j in range(dps - 1):
                sq_copy(k, j).start()

    def normalize(k):
        total = sq_out[k]
        for j in range(dps - 1):
            sq_copy(k, j).wait_recv()
            total = total + sq_in[j, k]
        mean_sq = jnp.sum(total, axis=1, keepdims=True) / (dps * cols)
        scale = jnp.where(row_mask(k), lax.rsqrt(mean_sq + 1e-06), 0.0)
        for n in range(tiles):
            at = pl.ds(n * tile, tile)
            g = gain[:, pl.ds(pl.multiple_of(dp * cols + n * tile, tile), tile)]
            normed[span(k), at] = (hidden[span(k), at] * scale * g).astype(jnp.bfloat16)

    def step(s, carry):
        @pl.when(s < steps)
        def _():
            gather(s)

        for n in range(tiles):

            @pl.when(s < steps)
            def _():
                product(s, n)
                if n > 0:
                    combine(s, n - 1)

            if n == 0:

                @pl.when((s > 0) & (s <= steps))
                def _():
                    combine(s - 1, tiles - 1)

            @pl.when((s > 0) & (s <= steps))
            def _():
                add_residual(s - 1, n)

        return carry

    lax.fori_loop(0, steps + 1, step, 0)

    def finish(k, carry):
        normalize(k)
        return carry

    lax.fori_loop(0, steps, finish, 0)

    def drain(k, carry):
        @pl.when(k > 0)
        def _():
            for j in range(dps - 1):
                y_copy(k, j).wait_send()

        for j in range(dps - 1):
            sq_copy(k, j).wait_send()
        for n in range(tiles):
            pair_copy(k, n).wait_send()
            for j in range(chips - 1):
                chip_copy(k, n, j).wait_send()

        @pl.when(sec < sections - 1)
        def _():
            for n in range(tiles):
                z_copy(k, n).wait_send()

        @pl.when(sec > 0)
        def _():
            for n in range(tiles):
                z_copy(k, n).wait_recv()

        return carry

    lax.fori_loop(0, steps, drain, 0)


def on_device(context, residual, out_weight, norm_gain, valid_tokens):
    sections, dps, tensors = (lax.axis_size(a) for a in ("section", "dp", "tensor"))
    chips = tensors // 2
    rows, cols = residual.shape[1:]
    local, depth = context.shape[1:]
    blocks = local // (2 * rows)
    assert blocks * dps == chips
    r = max(16, rows // PIECES)
    steps = rows // r
    tile = cols // GROUPS
    tiles = GROUPS
    sizes = (sections, dps, chips, blocks, rows, depth, cols, r, steps, tile)
    bf16, f32 = jnp.bfloat16, jnp.float32
    dma = pltpu.SemaphoreType.DMA
    total_rows = local * dps
    anywhere = pl.BlockSpec(memory_space=pl.ANY)
    out = pltpu.VMEM((rows, cols), bf16)
    normed, handoff = pl.pallas_call(
        functools.partial(relay_kernel, sizes),
        out_shape=(out, out),
        in_specs=[
            pl.BlockSpec(memory_space=pltpu.SMEM),
            anywhere,
            anywhere,
            anywhere,
            pl.BlockSpec(memory_space=pltpu.VMEM),
        ],
        out_specs=(pl.BlockSpec(memory_space=pltpu.VMEM),) * 2,
        scratch_shapes=[
            pltpu.VMEM((chips, 2, rows, depth), bf16),
            pltpu.VMEM((2 * chips * r, depth), bf16),
            pltpu.VMEM((depth, cols), bf16),
            pltpu.VMEM((rows, cols), bf16),
            pltpu.VMEM((chips, r, cols), f32),
            pltpu.VMEM((steps, chips, r, cols), bf16),
            pltpu.VMEM((steps, chips, r, cols), bf16),
            pltpu.VMEM((chips - 1, rows, cols), bf16),
            pltpu.VMEM((chips - 1, rows, cols), bf16),
            pltpu.VMEM((rows, cols), f32),
            pltpu.VMEM((rows, cols), bf16),
            pltpu.VMEM((steps, r, 128), f32),
            pltpu.VMEM((dps - 1, steps, r, 128), f32),
            dma,
            dma((tiles,)),
            dma,
            dma((steps, dps - 1)),
            dma((steps, dps - 1)),
            dma((steps, tiles)),
            dma((steps, tiles)),
            dma((steps, tiles, chips - 1)),
            dma((steps, tiles, chips - 1)),
            dma((steps, tiles)),
            dma((steps, tiles)),
            dma((steps, dps - 1)),
            dma((steps, dps - 1)),
        ],
        compiler_params=pltpu.CompilerParams(
            collective_id=0, has_side_effects=True, vmem_limit_bytes=56 * 2**20
        ),
        cost_estimate=pl.CostEstimate(
            flops=2 * total_rows * depth * cols,
            bytes_accessed=2 * (depth * cols + local * depth + 3 * rows * cols),
            transcendentals=0,
        ),
        name="relay",
    )(
        valid_tokens,
        context.reshape(blocks, 2, rows, depth),
        residual[0],
        out_weight[0],
        norm_gain,
    )
    return (normed[None], handoff[None])


def solution(mesh):
    placed = (
        P("section", "dp", "tensor"),
        P("section", "tensor", "dp"),
        P("section", "tensor", "dp"),
        P("section", None),
        P("section"),
    )
    return jax.shard_map(
        on_device,
        mesh=mesh,
        in_specs=placed,
        out_specs=(P("section", "tensor", "dp"), P("section", "tensor", "dp")),
        check_vma=False,
    )
```
